512 devices in a mesh: wide: 32 (over x, y_lo, core), narrow: 16 (over z, y_hi).
Axes of the slice: x: 4, y: 8 (y_hi: 2, y_lo: 4; y = y_hi * 4 + y_lo), z: 8, core: 2. Of those that a mesh axis runs over, the one named last changes fastest.
Arguments:
- query_act: bfloat16 [64, 16384], P(None, 'wide'), may hold values from -6 to 6
- query_grad: bfloat16 [64, 16384], P(None, 'narrow'), may hold values from -6 to 6
- act_basis: bfloat16 [16384, 16384], P('wide', 'narrow'), may hold values from -0.046875 to 0.046875
- grad_basis: bfloat16 [16384, 16384], P('narrow', 'wide'), may hold values from -0.046875 to 0.046875
- eigenvalues: float32 [16384, 16384], P('wide', 'narrow'), may hold values from 0.1 to 10
- train_act: bfloat16 [64, 16384], P(None, 'narrow'), may hold values from -6 to 6
- train_grad: bfloat16 [64, 16384], P(None, 'wide'), may hold values from -6 to 6
Outputs:
- scores: float32 [64, 64], replicated
The draws below stay inside these ranges and needn't reach their ends.
All inputs are finite; a program needn't handle non-finite values.
Results may differ from the reference program's by a relative error of at most 0.0057.
Values may be sent and summed in bfloat16 or wider, within the bound.
A program may use at most 64 MiB of HBM per device.

```python
import math
import jax
import jax.numpy as jnp
from jax import lax

A = 16384
G = 16384
Q = 64
TR = 64


def shard_levels(stream_key, extent, pieces, low, largest):
    level, own = 1.0, jax.random.fold_in(stream_key, 6)
    for axis_at, parts in pieces:
        heights = jnp.exp(jax.random.uniform(jax.random.fold_in(own, axis_at), (parts,), jnp.float32, low / len(pieces), largest / len(pieces)))
        level = level * jnp.repeat(heights, extent[axis_at] // parts).reshape([-1 if axis == axis_at else 1 for axis in range(len(extent))])
    return level


def scatter_about(key, dims, scale, bound, pieces=(), dtype=jnp.bfloat16):
    array = scale * jax.random.normal(key, dims, jnp.float32)
    if pieces:
        array = array * shard_levels(key, dims, pieces, -0.22, 0.18)
    return jnp.clip(array, -bound, bound).astype(dtype)


def setup_inputs(seed: int = 0) -> dict:
    keys = jax.random.split(jax.random.key(seed), 8)
    query_act = scatter_about(keys[0], (Q, A), 1.0, 6.0, ((1, 32),))
    query_grad = scatter_about(keys[1], (Q, G), 1.0, 6.0, ((1, 16),))
    act_basis = scatter_about(keys[2], (A, A), A ** -0.5, 0.046875, ((0, 32), (1, 16)))
    grad_basis = scatter_about(keys[3], (G, G), G ** -0.5, 0.046875, ((0, 16), (1, 32)))
    eigenvalues = jnp.clip(jnp.exp(math.log(10.0) - 4.6051702 * jax.random.uniform(keys[4], (G, A), jnp.float32) ** shard_levels(keys[4], (G, A), ((0, 32), (1, 16)), -0.2, 0.2)), 0.1, 10.0)
    train_act = scatter_about(keys[5], (TR, A), 1.0, 6.0, ((1, 16),))
    train_grad = scatter_about(keys[6], (TR, G), 1.0, 6.0, ((1, 32),))
    return {"query_act": query_act, "query_grad": query_grad, "act_basis": act_basis, "grad_basis": grad_basis, "eigenvalues": eigenvalues, "train_act": train_act, "train_grad": train_grad}


def reference(query_act, query_grad, act_basis, grad_basis, eigenvalues, train_act, train_grad):
    rot_act = jnp.dot(query_act, act_basis, preferred_element_type=jnp.float32).astype(jnp.bfloat16)
    rot_grad = jnp.dot(query_grad, grad_basis, preferred_element_type=jnp.float32).astype(jnp.bfloat16)
    inverse = lax.optimization_barrier((1.0 / eigenvalues).astype(jnp.bfloat16)).astype(jnp.float32)
    train_act32 = train_act.astype(jnp.float32)
    train_grad32 = train_grad.astype(jnp.float32)
    blocks_act = rot_act.reshape(Q // 8, 8, A)
    blocks_grad = rot_grad.reshape(Q // 8, 8, G)

    def one_block(items):
        block_act, block_grad = items
        pairs = (block_act.astype(jnp.float32)[:, None, :] * train_act32[None, :, :]).astype(jnp.bfloat16)
        pairs = lax.optimization_barrier(pairs).astype(jnp.float32)
        weighted = jnp.einsum("ij,btj->bti", inverse, pairs)
        factor = block_grad.astype(jnp.float32)[:, None, :] * train_grad32[None, :, :]
        return jnp.sum(weighted * factor, axis=2)

    totals = lax.map(one_block, (blocks_act, blocks_grad)).reshape(Q, TR)
    return totals * (float(A * G) ** -0.5)
```

```python
import jax
import jax.numpy as jnp
from jax import lax
from jax.experimental import pallas as pl
from jax.experimental.pallas import tpu as pltpu
from jax.sharding import PartitionSpec as P

A = 16384
G = 16384
BF = jnp.bfloat16
F32 = jnp.float32
MESH = pl.DeviceIdType.MESH

CA, CG, CT, CI, HR, HG, ZR, VV, ZG, AX, AY, AZ, FC = range(13)
N_EXCHANGES = 13


def kernel(
    qa_h, qg_h, ab_h, gb_h, eig_h, ta_h, tg_h,
    out,
    qa, qg, ab, gb, eig, ta, tg,
    inv, keep, ca_s, ca_r, ha_s, ha_r, rot_a, cg_s, zg_s, zg_r, vg_s, vg_r, rot_g,
    raf, rgf, tgf, pairs, accs, s0, s1, s2, s3, xr, yr, zr, fr,
    load, send, recv,
):
    w, n = lax.axis_index("wide"), lax.axis_index("narrow")
    x, yl, c = w // 8, lax.rem(w // 2, 4), lax.rem(w, 2)
    z, yh = n // 2, lax.rem(n, 2)
    chip = w // 2
    partner = (w + 1 - 2 * c, n)
    across = (w, n + 1 - 2 * yh)

    def chip_peer(d):
        return (lax.rem(chip + d, 16) * 2 + c, n)

    def x_peer(d):
        return (lax.rem(w + 8 * d, 32), n)

    def y_peer(d):
        y = lax.rem(yh * 4 + yl + d, 8)
        return (x * 8 + lax.rem(y, 4) * 2 + c, z * 2 + y // 4)

    def z_peer(d):
        return (w, lax.rem(n + 2 * d, 16))

    mine, other = pl.ds(pl.multiple_of(c * 32, 32), 32), pl.ds(pl.multiple_of(32 - c * 32, 32), 32)
    loads = [
        (qa_h.at[mine], qa.at[pl.ds(0, 32)]),
        (qa_h.at[other], qa.at[pl.ds(32, 32)]),
        (ab_h, ab),
        (qg_h.at[mine], qg.at[pl.ds(0, 32)]),
        (qg_h.at[other], qg.at[pl.ds(32, 32)]),
        (gb_h, gb),
        (tg_h, tg.at[0]),
        (eig_h, eig),
        (ta_h, ta),
    ]
    loads = [pltpu.make_async_copy(s, d, load.at[i]) for i, (s, d) in enumerate(loads)]
    for one in loads:
        one.start()

    barrier = pltpu.get_barrier_semaphore()

    @pl.loop(1, 8)
    def _(d):
        pl.semaphore_signal(barrier, inc=1, device_id=z_peer(d), device_id_type=MESH)

    pl.semaphore_signal(barrier, inc=1, device_id=across, device_id_type=MESH)

    @pl.loop(1, 16)
    def _(d):
        pl.semaphore_signal(barrier, inc=1, device_id=chip_peer(d), device_id_type=MESH)

    pl.semaphore_signal(barrier, inc=1, device_id=partner, device_id_type=MESH)

    def remote(src, dst, i, peer):
        pltpu.make_async_remote_copy(
            src, dst, send.at[i], recv.at[i], device_id=peer, device_id_type=MESH
        ).start()

    def await_bytes(ref, sem):
        pltpu.make_async_copy(ref, ref, sem).wait()

    for i in range(3):
        loads[i].wait()
    part = jnp.dot(qa[...], ab[...], preferred_element_type=F32)
    for k in range(16):
        rows, cols = 16 * (k // 8), slice(128 * (k % 8), 128 * (k % 8) + 128)
        keep[k] = part[rows : rows + 16, cols]
        ca_s[k] = part[rows + 32 : rows + 48, cols].astype(BF)
    pl.semaphore_wait(barrier, 24)
    remote(ca_s, ca_r, CA, partner)
    for i in range(3, 6):
        loads[i].wait()
    part = jnp.dot(qg[...], gb[...], preferred_element_type=F32)
    for k in range(8):
        rows, cols = 16 * (k // 4), slice(128 * (k % 4), 128 * (k % 4) + 128)
        zg_s[k] = part[rows : rows + 16, cols].astype(BF)
        cg_s[k] = part[rows + 32 : rows + 48, cols].astype(BF)
    remote(cg_s, zg_s.at[pl.ds(8, 8)], CG, partner)

    await_bytes(ca_r, recv.at[CA])
    ha_s[...] = (keep[...] + ca_r[...].astype(F32)).astype(BF)

    @pl.loop(1, 16)
    def _(d):
        remote(ha_s.at[lax.rem(chip + d, 16)], ha_r.at[d - 1], HR, chip_peer(d))

    await_bytes(cg_s, recv.at[CG])

    @pl.loop(1, 8)
    def _(d):
        remote(zg_s.at[pl.ds(2 * lax.rem(z + d, 8), 2)], zg_r.at[d - 1], ZR, z_peer(d))

    loads[6].wait()
    remote(tg.at[0], tg.at[1], CT, partner)
    loads[7].wait()
    for k in range(2):
        inv[k] = (1.0 / eig[pl.ds(256 * k, 256), :]).astype(BF)
    remote(inv.at[pl.ds(0, 2)], inv.at[pl.ds(2, 2)], CI, partner)
    loads[8].wait()

    await_bytes(ha_r, recv.at[HR])
    rot_a[chip] = (ha_s[chip].astype(F32) + jnp.sum(ha_r[...].astype(F32), axis=0)).astype(BF)

    @pl.loop(1, 16)
    def _(d):
        remote(rot_a.at[chip], rot_a.at[chip], HG, chip_peer(d))

    await_bytes(zg_r, recv.at[ZR])
    own = pl.ds(2 * z, 2)
    total = zg_s[own].astype(F32) + jnp.sum(zg_r[...].astype(F32), axis=0)
    vg_s[...] = total.astype(BF)
    remote(vg_s, vg_r, VV, across)
    await_bytes(vg_r, recv.at[VV])
    rot_g[own] = (total + vg_r[...].astype(F32)).astype(BF)

    @pl.loop(1, 8)
    def _(d):
        remote(rot_g.at[own], rot_g.at[own], ZG, z_peer(d))

    await_bytes(tg.at[0], recv.at[CT])
    for k in range(2):
        tgf[:, 512 * k : 512 * k + 512] = tg[k].astype(F32)

    await_bytes(rot_a.at[pl.ds(0, 15)], recv.at[HG])
    for k in range(16):
        raf[16 * (k // 8) : 16 * (k // 8) + 16, 128 * (k % 8) : 128 * (k % 8) + 128] = rot_a[k].astype(F32)

    @pl.loop(0, 4)
    def _(b):
        for k in range(8):
            row = raf[pl.ds(b * 8 + k, 1), :]
            at = pl.multiple_of(b * 512 + k * 64, 64)
            for j in range(8):
                cols = slice(128 * j, 128 * j + 128)
                wide_row = jnp.broadcast_to(row[:, cols], (16, 128)).astype(BF)
                for t in range(4):
                    pairs[pl.ds(at + 16 * t, 16), cols] = wide_row * ta[16 * t : 16 * t + 16, cols]

    await_bytes(inv.at[pl.ds(0, 2)], recv.at[CI])
    await_bytes(rot_g.at[pl.ds(0, 14)], recv.at[ZG])
    for k in range(16):
        rows, cols = 16 * (k // 4 % 2), 512 * (k // 8) + 128 * (k % 4)
        rgf[rows : rows + 16, cols : cols + 128] = rot_g[k].astype(F32)

    accs[...] = jnp.zeros_like(accs)

    @pl.loop(0, 4)
    def _(b):
        weighted = lax.dot_general(
            pairs[...], inv[b], (((1,), (1,)), ((), ())), preferred_element_type=F32
        )
        cols = pl.ds(pl.multiple_of(b * 256, 256), 256)
        train = tgf[:, cols]
        for k in range(32):
            rows = slice(64 * k, 64 * k + 64)
            terms = weighted[rows] * train * rgf[pl.ds(k, 1), cols]
            accs[rows, :] += terms[:, :128] + terms[:, 128:]

    ones = jnp.ones((8, 128), BF)
    high = accs[...].astype(BF)
    low = (accs[...] - high.astype(F32)).astype(BF)
    last = (((1,), (1,)), ((), ()))
    sums = lax.dot_general(ones, high, last, preferred_element_type=F32) + lax.dot_general(
        ones, low, last, preferred_element_type=F32
    )
    for k in range(16):
        s0[k : k + 1, :] = sums[0:1, 128 * k : 128 * k + 128]

    for d in range(1, 4):
        remote(s0, xr.at[d - 1], AX, x_peer(d))
    await_bytes(xr, recv.at[AX])
    s1[...] = s0[...] + jnp.sum(xr[...], axis=0)

    @pl.loop(1, 8)
    def _(d):
        remote(s1, yr.at[d - 1], AY, y_peer(d))

    await_bytes(yr, recv.at[AY])
    s2[...] = s1[...] + jnp.sum(yr[...], axis=0)

    @pl.loop(1, 8)
    def _(d):
        remote(s2, zr.at[d - 1], AZ, z_peer(d))

    await_bytes(zr, recv.at[AZ])
    s3[...] = s2[...] + jnp.sum(zr[...], axis=0)
    remote(s3, fr, FC, partner)
    await_bytes(fr, recv.at[FC])
    out[c] = s3[...]
    out[1 - c] = fr[...]

    sent = {
        CA: ca_s, CG: cg_s, CT: tg.at[0], CI: inv.at[pl.ds(0, 2)], HR: ha_r, HG: ha_r, ZR: zg_r,
        VV: vg_s, ZG: rot_g.at[pl.ds(0, 14)], AX: xr, AY: yr, AZ: zr, FC: fr,
    }
    for i, ref in sent.items():
        await_bytes(ref, send.at[i])


def on_device(*operands):
    vm = pltpu.VMEM
    scratch = [
        vm((64, 512), BF), vm((64, 1024), BF), vm((512, 1024), BF), vm((1024, 512), BF),
        vm((512, 1024), F32), vm((64, 1024), BF), vm((2, 64, 512), BF),
        vm((4, 256, 1024), BF), vm((16, 16, 128), F32), vm((16, 16, 128), BF), vm((16, 16, 128), BF),
        vm((16, 16, 128), BF), vm((15, 16, 128), BF), vm((16, 16, 128), BF),
        vm((8, 16, 128), BF), vm((16, 16, 128), BF), vm((7, 2, 16, 128), BF),
        vm((2, 16, 128), BF), vm((2, 16, 128), BF), vm((16, 16, 128), BF),
        vm((32, 1024), F32), vm((32, 1024), F32), vm((64, 1024), F32),
        vm((2048, 1024), BF), vm((2048, 128), F32),
        vm((16, 128), F32), vm((16, 128), F32), vm((16, 128), F32), vm((16, 128), F32),
        vm((3, 16, 128), F32), vm((7, 16, 128), F32), vm((7, 16, 128), F32), vm((16, 128), F32),
        pltpu.SemaphoreType.DMA((9,)),
        pltpu.SemaphoreType.DMA((N_EXCHANGES,)),
        pltpu.SemaphoreType.DMA((N_EXCHANGES,)),
    ]
    scores = pl.pallas_call(
        kernel,
        out_shape=jax.ShapeDtypeStruct((2, 16, 128), F32),
        in_specs=[pl.BlockSpec(memory_space=pl.ANY)] * 7,
        out_specs=pl.BlockSpec(memory_space=pltpu.VMEM),
        scratch_shapes=scratch,
        compiler_params=pltpu.CompilerParams(
            collective_id=0, has_side_effects=True, vmem_limit_bytes=60 * 2**20
        ),
        name="influence",
    )(*operands)
    return scores.reshape(64, 64) * float(A * G) ** (-0.5)


def solution(mesh):
    in_specs = (
        P(None, "wide"),
        P(None, "narrow"),
        P("wide", "narrow"),
        P("narrow", "wide"),
        P("wide", "narrow"),
        P(None, "narrow"),
        P(None, "wide"),
    )
    return jax.shard_map(on_device, mesh=mesh, in_specs=in_specs, out_specs=P(), check_vma=False)
```

```python
import jax
import jax.numpy as jnp
from jax import lax
from jax.experimental import pallas as pl
from jax.experimental.pallas import tpu as pltpu
from jax.sharding import PartitionSpec as P

A = 16384
G = 16384
BF = jnp.bfloat16
F32 = jnp.float32
MESH = pl.DeviceIdType.MESH

CA, CG, CT, CI, HR, HG, ZR, NG, AX, AY, AZ, FC = range(12)
N_EXCHANGES = 12
RING4 = (2, 1, 3)
RING8 = (4, 3, 5, 2, 6, 1, 7)


def kernel(
    qa_h, qg_h, ab_h, gb_h, eig_h, ta_h, tg_h,
    out,
    qa, qg, ab, gb, eig, ta, tg,
    inv, keep, ca_s, ca_r, ha_s, ha_r, rot_a, cg_s, zg_s, zg_r, rot_g,
    raf, rgf, tgf, pairs, first, accs, s0, s1, s2, s3, xr, yr, zr, fr,
    load, send, recv, ready,
):
    w, n = lax.axis_index("wide"), lax.axis_index("narrow")
    x, yl, c = w // 8, lax.rem(w // 2, 4), lax.rem(w, 2)
    z, yh = n // 2, lax.rem(n, 2)
    chip = w // 2
    partner = (w + 1 - 2 * c, n)
    across = (w, n + 1 - 2 * yh)

    owner = (yl == 1) | (yl == 2)

    def chip_at(dx, to_yl):
        return (lax.rem(x + dx, 4) * 8 + to_yl * 2 + c, n)

    def y_peer(d):
        y = lax.rem(yh * 4 + yl + d, 8)
        return (x * 8 + lax.rem(y, 4) * 2 + c, z * 2 + y // 4)

    def z_peer(d):
        return (w, lax.rem(n + 2 * d, 16))

    def narrow_peer(dz, dy):
        return (w, lax.rem(z + dz, 8) * 2 + lax.rem(yh + dy, 2))

    mine, other = pl.ds(pl.multiple_of(c * 32, 32), 32), pl.ds(pl.multiple_of(32 - c * 32, 32), 32)
    loads = [
        (qa_h.at[mine], qa.at[pl.ds(0, 32)]),
        (qa_h.at[other], qa.at[pl.ds(32, 32)]),
        (ab_h, ab),
        (qg_h.at[mine], qg.at[pl.ds(0, 32)]),
        (qg_h.at[other], qg.at[pl.ds(32, 32)]),
        (gb_h, gb),
        (tg_h, tg.at[0]),
        (eig_h, eig),
        (ta_h, ta),
    ]
    loads = [pltpu.make_async_copy(s, d, load.at[i]) for i, (s, d) in enumerate(loads)]
    for one in loads:
        one.start()

    barrier = pltpu.get_barrier_semaphore()

    def greet(peer):
        pl.semaphore_signal(barrier, inc=1, device_id=peer, device_id_type=MESH)

    for d in RING8:
        greet(z_peer(d))
    for d in RING4 + (0,):
        for e in (2, 1, 3, 0):
            if d or e:
                greet(chip_at(d, lax.rem(yl + e, 4)))
    greet(across)
    for e in (2, 1, 3):
        greet((w + 2 * (lax.rem(yl + e, 4) - yl), n + 1 - 2 * yh))
    greet(partner)

    def remote(src, dst, i, peer):
        pltpu.make_async_remote_copy(
            src, dst, send.at[i], recv.at[i], device_id=peer, device_id_type=MESH
        ).start()

    def await_bytes(ref, sem):
        pltpu.make_async_copy(ref, ref, sem).wait()

    for i in range(3):
        loads[i].wait()
    part = jnp.dot(qa[...], ab[...], preferred_element_type=F32)
    for k in range(16):
        rows, cols = 16 * (k // 8), slice(128 * (k % 8), 128 * (k % 8) + 128)
        keep[k] = part[rows : rows + 16, cols]
        ca_s[k] = part[rows + 32 : rows + 48, cols].astype(BF)
    pl.semaphore_wait(barrier, 27)
    pl.semaphore_signal(ready, inc=1, device_id=across, device_id_type=MESH)
    remote(ca_s, ca_r, CA, partner)
    for i in range(3, 6):
        loads[i].wait()
    part = jnp.dot(qg[...], gb[...], preferred_element_type=F32)
    for k in range(8):
        rows, cols = 16 * (k // 4), slice(128 * (k % 4), 128 * (k % 4) + 128)
        zg_s[k] = part[rows : rows + 16, cols].astype(BF)
        cg_s[k] = part[rows + 32 : rows + 48, cols].astype(BF)
    remote(cg_s, zg_s.at[pl.ds(8, 8)], CG, partner)

    await_bytes(ca_r, recv.at[CA])
    ha_s[...] = (keep[...] + ca_r[...].astype(F32)).astype(BF)
    for d in RING4 + (0,):
        for to in (1, 2):

            def to_owner(d=d, to=to):
                at = pl.ds(4 * lax.rem(x + d, 4) + 2 * to - 2, 2)
                slot = 4 * ((4 - d) % 4) + lax.rem(yl - to + 4, 4) - 1
                remote(ha_s.at[at], ha_r.at[slot], HR, chip_at(d, to))

            if d:
                to_owner()
            else:
                pl.when(yl != to)(to_owner)

    await_bytes(cg_s, recv.at[CG])
    for d in RING8:
        remote(zg_s.at[pl.ds(2 * lax.rem(z + d, 8), 2)], zg_r.at[d - 1], ZR, z_peer(d))

    loads[6].wait()
    remote(tg.at[0], tg.at[1], CT, partner)
    loads[7].wait()
    for k in range(2):
        inv[k] = (1.0 / eig[pl.ds(256 * k, 256), :]).astype(BF)
    remote(inv.at[pl.ds(0, 2)], inv.at[pl.ds(2, 2)], CI, partner)
    loads[8].wait()

    @pl.when(owner)
    def _():
        await_bytes(ha_r, recv.at[HR])
        at = pl.ds(4 * x + 2 * yl - 2, 2)
        rot_a[at] = (ha_s[at].astype(F32) + jnp.sum(ha_r[...].astype(F32), axis=0)).astype(BF)
        for d in RING4 + (0,):
            for e in (2, 1, 3, 0):
                if d or e:
                    remote(rot_a.at[at], rot_a.at[at], HG, chip_at(d, lax.rem(yl + e, 4)))

    await_bytes(zg_r, recv.at[ZR])
    own = pl.ds(2 * z, 2)
    held = pl.ds(16 * yh + 2 * z, 2)
    rot_g[held] = (zg_s[own].astype(F32) + jnp.sum(zg_r[...].astype(F32), axis=0)).astype(BF)
    pl.semaphore_wait(ready, 1)
    for e in (1, 0):
        for d in RING8 + (0,):
            if d or e:
                remote(rot_g.at[held], rot_g.at[held], NG, narrow_peer(d, e))

    await_bytes(tg.at[0], recv.at[CT])
    for k in range(2):
        tgf[:, 512 * k : 512 * k + 512] = tg[k].astype(F32)

    @pl.when(owner)
    def _():
        await_bytes(rot_a.at[pl.ds(0, 14)], recv.at[HG])

    @pl.when(jnp.logical_not(owner))
    def _():
        await_bytes(rot_a, recv.at[HG])

    for k in range(16):
        raf[16 * (k // 8) : 16 * (k // 8) + 16, 128 * (k % 8) : 128 * (k % 8) + 128] = rot_a[k].astype(F32)

    @pl.loop(0, 4)
    def _(b):
        for k in range(8):
            row = raf[pl.ds(b * 8 + k, 1), :]
            at = pl.multiple_of(b * 512 + k * 64, 64)
            for j in range(8):
                cols = slice(128 * j, 128 * j + 128)
                wide_row = jnp.broadcast_to(row[:, cols], (16, 128)).astype(BF)
                for t in range(4):
                    pairs[pl.ds(at + 16 * t, 16), cols] = wide_row * ta[16 * t : 16 * t + 16, cols]

    await_bytes(inv.at[pl.ds(0, 2)], recv.at[CI])

    def product(b):
        return lax.dot_general(
            pairs[...], inv[b], (((1,), (1,)), ((), ())), preferred_element_type=F32
        )

    def add_terms(b, weighted):
        cols = pl.ds(pl.multiple_of(b * 256, 256), 256)
        train = tgf[:, cols]
        for k in range(32):
            rows = slice(64 * k, 64 * k + 64)
            terms = weighted[rows] * train * rgf[pl.ds(k, 1), cols]
            accs[rows, :] += terms[:, :128] + terms[:, 128:]

    first[...] = product(0)
    await_bytes(rot_g.at[pl.ds(0, 30)], recv.at[NG])
    for k in range(16):
        rows, cols = 16 * (k // 4 % 2), 512 * (k // 8) + 128 * (k % 4)
        both = rot_g[k].astype(F32) + rot_g[16 + k].astype(F32)
        rgf[rows : rows + 16, cols : cols + 128] = both.astype(BF).astype(F32)

    accs[...] = jnp.zeros_like(accs)
    add_terms(0, first)

    @pl.loop(1, 4)
    def _(b):
        add_terms(b, product(b))

    ones = jnp.ones((8, 128), BF)
    high = accs[...].astype(BF)
    low = (accs[...] - high.astype(F32)).astype(BF)
    last = (((1,), (1,)), ((), ()))
    sums = lax.dot_general(ones, high, last, preferred_element_type=F32) + lax.dot_general(
        ones, low, last, preferred_element_type=F32
    )
    for k in range(16):
        s0[k : k + 1, :] = sums[0:1, 128 * k : 128 * k + 128]

    for d in RING4:
        remote(s0, xr.at[d - 1], AX, chip_at(d, yl))
    await_bytes(xr, recv.at[AX])
    s1[...] = s0[...] + jnp.sum(xr[...], axis=0)

    for d in RING8:
        remote(s1, yr.at[d - 1], AY, y_peer(d))

    await_bytes(yr, recv.at[AY])
    s2[...] = s1[...] + jnp.sum(yr[...], axis=0)

    for d in RING8:
        remote(s2, zr.at[d - 1], AZ, z_peer(d))

    await_bytes(zr, recv.at[AZ])
    s3[...] = (s2[...] + jnp.sum(zr[...], axis=0)) * float(A * G) ** (-0.5)
    remote(s3, fr, FC, partner)
    await_bytes(fr, recv.at[FC])
    for half, ref in ((c, s3), (1 - c, fr)):
        for k in range(32):
            out[pl.ds(32 * half + k, 1), :] = ref[k // 2 : k // 2 + 1, 64 * (k % 2) : 64 * (k % 2) + 64]

    sent = {
        CA: ca_s, CG: cg_s, CT: tg.at[0], CI: inv.at[pl.ds(0, 2)], ZR: zg_r,
        AX: xr, AY: yr, AZ: zr, FC: fr,
    }
    for i, ref in sent.items():
        await_bytes(ref, send.at[i])
    await_bytes(rot_g.at[pl.ds(0, 30)], send.at[NG])

    @pl.when(owner)
    def _():
        await_bytes(ha_s.at[pl.ds(0, 14)], send.at[HR])
        await_bytes(ha_r, send.at[HG])

    @pl.when(jnp.logical_not(owner))
    def _():
        await_bytes(ha_s, send.at[HR])


def on_device(*operands):
    vm = pltpu.VMEM
    scratch = [
        vm((64, 512), BF), vm((64, 1024), BF), vm((512, 1024), BF), vm((1024, 512), BF),
        vm((512, 1024), F32), vm((64, 1024), BF), vm((2, 64, 512), BF),
        vm((4, 256, 1024), BF), vm((16, 16, 128), F32), vm((16, 16, 128), BF), vm((16, 16, 128), BF),
        vm((16, 16, 128), BF), vm((15, 2, 16, 128), BF), vm((16, 16, 128), BF),
        vm((8, 16, 128), BF), vm((16, 16, 128), BF), vm((7, 2, 16, 128), BF),
        vm((32, 16, 128), BF),
        vm((32, 1024), F32), vm((32, 1024), F32), vm((64, 1024), F32),
        vm((2048, 1024), BF), vm((2048, 256), F32), vm((2048, 128), F32),
        vm((16, 128), F32), vm((16, 128), F32), vm((16, 128), F32), vm((16, 128), F32),
        vm((3, 16, 128), F32), vm((7, 16, 128), F32), vm((7, 16, 128), F32), vm((16, 128), F32),
        pltpu.SemaphoreType.DMA((9,)),
        pltpu.SemaphoreType.DMA((N_EXCHANGES,)),
        pltpu.SemaphoreType.DMA((N_EXCHANGES,)),
        pltpu.SemaphoreType.REGULAR,
    ]
    return pl.pallas_call(
        kernel,
        out_shape=jax.ShapeDtypeStruct((64, 64), F32),
        in_specs=[pl.BlockSpec(memory_space=pl.ANY)] * 7,
        out_specs=pl.BlockSpec(memory_space=pltpu.VMEM),
        scratch_shapes=scratch,
        compiler_params=pltpu.CompilerParams(
            collective_id=0, has_side_effects=True, vmem_limit_bytes=60 * 2**20
        ),
        name="influence",
    )(*operands)


def solution(mesh):
    in_specs = (
        P(None, "wide"),
        P(None, "narrow"),
        P("wide", "narrow"),
        P("narrow", "wide"),
        P("wide", "narrow"),
        P(None, "narrow"),
        P(None, "wide"),
    )
    return jax.shard_map(on_device, mesh=mesh, in_specs=in_specs, out_specs=P(), check_vma=False)
```

```python
import jax
import jax.numpy as jnp
from jax import lax
from jax.experimental import pallas as pl
from jax.experimental.pallas import tpu as pltpu
from jax.sharding import PartitionSpec as P

A = 16384
G = 16384
BF = jnp.bfloat16
F32 = jnp.float32
MESH = pl.DeviceIdType.MESH

CA, CG, CT, CI, HR, HG, ZR, NG, AX, AY, AZ, FC = range(12)
N_EXCHANGES = 12
RING4 = (2, 1, 3)
RING8 = (4, 3, 5, 2, 6, 1, 7)


def kernel(
    qa_h, qg_h, ab_h, gb_h, eig_h, ta_h, tg_h,
    out,
    qa, qg, ab, gb, eig, ta, tg,
    inv, keep, ca_s, ca_r, ha_s, ha_r, rot_a, cg_s, zg_s, zg_r, rot_g,
    raf, rgf, tgf, pairs, first, accs, s0, s1, s2, s3, xr, yr, zr, fr,
    load, send, recv, ready,
):
    w, n = lax.axis_index("wide"), lax.axis_index("narrow")
    x, yl, c = w // 8, lax.rem(w // 2, 4), lax.rem(w, 2)
    z, yh = n // 2, lax.rem(n, 2)
    chip = w // 2
    partner = (w + 1 - 2 * c, n)
    across = (w, n + 1 - 2 * yh)

    owner = (yl == 1) | (yl == 2)

    def chip_at(dx, to_yl):
        return (lax.rem(x + dx, 4) * 8 + to_yl * 2 + c, n)

    def y_peer(d):
        y = lax.rem(yh * 4 + yl + d, 8)
        return (x * 8 + lax.rem(y, 4) * 2 + c, z * 2 + y // 4)

    def z_peer(d):
        return (w, lax.rem(n + 2 * d, 16))

    def narrow_peer(dz, dy):
        return (w, lax.rem(z + dz, 8) * 2 + lax.rem(yh + dy, 2))

    mine, other = pl.ds(pl.multiple_of(c * 32, 32), 32), pl.ds(pl.multiple_of(32 - c * 32, 32), 32)
    loads = [
        (qa_h.at[mine], qa.at[pl.ds(0, 32)]),
        (qa_h.at[other], qa.at[pl.ds(32, 32)]),
        (ab_h, ab),
        (qg_h.at[mine], qg.at[pl.ds(0, 32)]),
        (qg_h.at[other], qg.at[pl.ds(32, 32)]),
        (gb_h, gb),
        (tg_h, tg.at[0]),
        (eig_h, eig),
        (ta_h, ta),
    ]
    loads = [pltpu.make_async_copy(s, d, load.at[i]) for i, (s, d) in enumerate(loads)]
    for one in loads[:3]:
        one.start()

    barrier = pltpu.get_barrier_semaphore()

    def greet(peer):
        pl.semaphore_signal(barrier, inc=1, device_id=peer, device_id_type=MESH)

    for d in RING8:
        greet(z_peer(d))
    for d in RING4 + (0,):
        for e in (2, 1, 3, 0):
            if d or e:
                greet(chip_at(d, lax.rem(yl + e, 4)))
    greet(across)
    for e in (2, 1, 3):
        greet((w + 2 * (lax.rem(yl + e, 4) - yl), n + 1 - 2 * yh))
    greet(partner)

    def remote(src, dst, i, peer):
        pltpu.make_async_remote_copy(
            src, dst, send.at[i], recv.at[i], device_id=peer, device_id_type=MESH
        ).start()

    def await_bytes(ref, sem):
        pltpu.make_async_copy(ref, ref, sem).wait()

    for i in range(3):
        loads[i].wait()
    for one in loads[3:]:
        one.start()
    part = jnp.dot(qa[...], ab[...], preferred_element_type=F32)
    for k in range(16):
        rows, cols = 16 * (k // 8), slice(128 * (k % 8), 128 * (k % 8) + 128)
        keep[k] = part[rows : rows + 16, cols]
        ca_s[k] = part[rows + 32 : rows + 48, cols].astype(BF)
    pl.semaphore_wait(barrier, 27)
    remote(ca_s, ca_r, CA, partner)
    pl.semaphore_signal(ready, inc=1, device_id=across, device_id_type=MESH)
    for i in range(3, 6):
        loads[i].wait()
    part = jnp.dot(qg[...], gb[...], preferred_element_type=F32)
    for k in range(8):
        rows, cols = 16 * (k // 4), slice(128 * (k % 4), 128 * (k % 4) + 128)
        zg_s[k] = part[rows : rows + 16, cols].astype(BF)
        cg_s[k] = part[rows + 32 : rows + 48, cols].astype(BF)
    remote(cg_s, zg_s.at[pl.ds(8, 8)], CG, partner)
    await_bytes(ca_r, recv.at[CA])
    ha_s[...] = (keep[...] + ca_r[...].astype(F32)).astype(BF)
    for d in RING4 + (0,):
        for to in (1, 2):

            def to_owner(d=d, to=to):
                at = pl.ds(4 * lax.rem(x + d, 4) + 2 * to - 2, 2)
                slot = 4 * ((4 - d) % 4) + lax.rem(yl - to + 4, 4) - 1
                remote(ha_s.at[at], ha_r.at[slot], HR, chip_at(d, to))

            if d:
                to_owner()
            else:
                pl.when(yl != to)(to_owner)

    await_bytes(cg_s, recv.at[CG])
    for d in RING8:
        remote(zg_s.at[pl.ds(2 * lax.rem(z + d, 8), 2)], zg_r.at[d - 1], ZR, z_peer(d))

    loads[6].wait()
    remote(tg.at[0], tg.at[1], CT, partner)
    loads[7].wait()
    for k in range(2):
        inv[k] = (1.0 / eig[pl.ds(256 * k, 256), :]).astype(BF)
    remote(inv.at[pl.ds(0, 2)], inv.at[pl.ds(2, 2)], CI, partner)
    loads[8].wait()

    @pl.when(owner)
    def _():
        await_bytes(ha_r, recv.at[HR])
        at = pl.ds(4 * x + 2 * yl - 2, 2)
        rot_a[at] = (ha_s[at].astype(F32) + jnp.sum(ha_r[...].astype(F32), axis=0)).astype(BF)
        for d in RING4 + (0,):
            for e in (2, 1, 3, 0):
                if d or e:
                    remote(rot_a.at[at], rot_a.at[at], HG, chip_at(d, lax.rem(yl + e, 4)))

    await_bytes(zg_r, recv.at[ZR])
    own = pl.ds(2 * z, 2)
    held = pl.ds(16 * yh + 2 * z, 2)
    rot_g[held] = (zg_s[own].astype(F32) + jnp.sum(zg_r[...].astype(F32), axis=0)).astype(BF)
    pl.semaphore_wait(ready, 1)
    for e in (1, 0):
        for d in RING8 + (0,):
            if d or e:
                remote(rot_g.at[held], rot_g.at[held], NG, narrow_peer(d, e))

    await_bytes(tg.at[0], recv.at[CT])
    for k in range(2):
        tgf[:, 512 * k : 512 * k + 512] = tg[k].astype(F32)

    @pl.when(owner)
    def _():
        await_bytes(rot_a.at[pl.ds(0, 14)], recv.at[HG])

    @pl.when(jnp.logical_not(owner))
    def _():
        await_bytes(rot_a, recv.at[HG])

    for k in range(16):
        raf[16 * (k // 8) : 16 * (k // 8) + 16, 128 * (k % 8) : 128 * (k % 8) + 128] = rot_a[k].astype(F32)

    @pl.loop(0, 4)
    def _(b):
        for k in range(8):
            row = raf[pl.ds(b * 8 + k, 1), :]
            at = pl.multiple_of(b * 512 + k * 64, 64)
            for j in range(8):
                cols = slice(128 * j, 128 * j + 128)
                wide_row = jnp.broadcast_to(row[:, cols], (16, 128)).astype(BF)
                for t in range(4):
                    pairs[pl.ds(at + 16 * t, 16), cols] = wide_row * ta[16 * t : 16 * t + 16, cols]

    await_bytes(inv.at[pl.ds(0, 2)], recv.at[CI])

    def product(b):
        return lax.dot_general(
            pairs[...], inv[b], (((1,), (1,)), ((), ())), preferred_element_type=F32
        )

    @pl.loop(0, 3)
    def _(b):
        first[b] = product(b)

    await_bytes(rot_g.at[pl.ds(0, 30)], recv.at[NG])
    for k in range(16):
        rows, cols = 16 * (k // 4 % 2), 512 * (k // 8) + 128 * (k % 4)
        both = rot_g[k].astype(F32) + rot_g[16 + k].astype(F32)
        rgf[rows : rows + 16, cols : cols + 128] = both.astype(BF).astype(F32)

    final = product(3)
    for k in range(32):
        rows = slice(64 * k, 64 * k + 64)
        total = None
        for b in range(4):
            cols = slice(256 * b, 256 * b + 256)
            terms = (first[b, rows] if b < 3 else final[rows]) * tgf[:, cols] * rgf[k : k + 1, cols]
            terms = terms[:, :128] + terms[:, 128:]
            total = terms if total is None else total + terms
        accs[rows, :] = total

    ones = jnp.ones((8, 128), BF)
    high = accs[...].astype(BF)
    low = (accs[...] - high.astype(F32)).astype(BF)
    last = (((1,), (1,)), ((), ()))
    sums = lax.dot_general(ones, high, last, preferred_element_type=F32) + lax.dot_general(
        ones, low, last, preferred_element_type=F32
    )
    for k in range(16):
        s0[k : k + 1, :] = sums[0:1, 128 * k : 128 * k + 128]

    for d in RING4:
        remote(s0, xr.at[d - 1], AX, chip_at(d, yl))
    await_bytes(xr, recv.at[AX])
    s1[...] = s0[...] + jnp.sum(xr[...], axis=0)

    for d in RING8:
        remote(s1, yr.at[d - 1], AY, y_peer(d))

    await_bytes(yr, recv.at[AY])
    s2[...] = s1[...] + jnp.sum(yr[...], axis=0)

    for d in RING8:
        remote(s2, zr.at[d - 1], AZ, z_peer(d))

    await_bytes(zr, recv.at[AZ])
    s3[...] = (s2[...] + jnp.sum(zr[...], axis=0)) * float(A * G) ** (-0.5)
    remote(s3, fr, FC, partner)
    await_bytes(fr, recv.at[FC])
    out[pl.ds(pl.multiple_of(16 * c, 16), 16), :] = s3[...]
    out[pl.ds(pl.multiple_of(16 - 16 * c, 16), 16), :] = fr[...]

    sent = {
        CA: ca_s, CG: cg_s, CT: tg.at[0], CI: inv.at[pl.ds(0, 2)], ZR: zg_r,
        AX: xr, AY: yr, AZ: zr, FC: fr,
    }
    for i, ref in sent.items():
        await_bytes(ref, send.at[i])
    await_bytes(rot_g.at[pl.ds(0, 30)], send.at[NG])

    @pl.when(owner)
    def _():
        await_bytes(ha_s.at[pl.ds(0, 14)], send.at[HR])
        await_bytes(ha_r, send.at[HG])

    @pl.when(jnp.logical_not(owner))
    def _():
        await_bytes(ha_s, send.at[HR])


def on_device(*operands):
    vm = pltpu.VMEM
    scratch = [
        vm((64, 512), BF), vm((64, 1024), BF), vm((512, 1024), BF), vm((1024, 512), BF),
        vm((512, 1024), F32), vm((64, 1024), BF), vm((2, 64, 512), BF),
        vm((4, 256, 1024), BF), vm((16, 16, 128), F32), vm((16, 16, 128), BF), vm((16, 16, 128), BF),
        vm((16, 16, 128), BF), vm((15, 2, 16, 128), BF), vm((16, 16, 128), BF),
        vm((8, 16, 128), BF), vm((16, 16, 128), BF), vm((7, 2, 16, 128), BF),
        vm((32, 16, 128), BF),
        vm((32, 1024), F32), vm((32, 1024), F32), vm((64, 1024), F32),
        vm((2048, 1024), BF), vm((3, 2048, 256), F32), vm((2048, 128), F32),
        vm((16, 128), F32), vm((16, 128), F32), vm((16, 128), F32), vm((16, 128), F32),
        vm((3, 16, 128), F32), vm((7, 16, 128), F32), vm((7, 16, 128), F32), vm((16, 128), F32),
        pltpu.SemaphoreType.DMA((9,)),
        pltpu.SemaphoreType.DMA((N_EXCHANGES,)),
        pltpu.SemaphoreType.DMA((N_EXCHANGES,)),
        pltpu.SemaphoreType.REGULAR,
    ]
    scores = pl.pallas_call(
        kernel,
        out_shape=jax.ShapeDtypeStruct((32, 128), F32),
        in_specs=[pl.BlockSpec(memory_space=pl.ANY)] * 7,
        out_specs=pl.BlockSpec(memory_space=pltpu.VMEM),
        scratch_shapes=scratch,
        compiler_params=pltpu.CompilerParams(
            collective_id=0, has_side_effects=True, vmem_limit_bytes=60 * 2**20
        ),
        name="influence",
    )(*operands)
    return scores.reshape(64, 64)


def solution(mesh):
    in_specs = (
        P(None, "wide"),
        P(None, "narrow"),
        P("wide", "narrow"),
        P("narrow", "wide"),
        P("wide", "narrow"),
        P(None, "narrow"),
        P(None, "wide"),
    )
    return jax.shard_map(on_device, mesh=mesh, in_specs=in_specs, out_specs=P(), check_vma=False)
```

```python
import jax
import jax.numpy as jnp
from jax import lax
from jax.experimental import pallas as pl
from jax.experimental.pallas import tpu as pltpu
from jax.sharding import PartitionSpec as P

A = 16384
G = 16384
BF = jnp.bfloat16
F32 = jnp.float32
MESH = pl.DeviceIdType.MESH

CA, CG, CT, CI, HR, HG, ZR, NG, AX, AY, AZ, FC = range(12)
N_EXCHANGES = 12
RING4 = (2, 1, 3)
RING8 = (4, 3, 5, 2, 6, 1, 7)


def kernel(
    qa_h, qg_h, ab_h, gb_h, eig_h, ta_h, tg_h,
    out,
    qa, qg, ab, gb, eig, ta, tg,
    inv, keep, ca_s, ca_r, ha_s, ha_r, rot_a, cg_s, zg_s, zg_r, rot_g,
    raf, rgf, tgf, pairs, first, accs, s0, s1, s2, s3, xr, yr, zr, fr,
    load, send, recv, ready,
):
    w, n = lax.axis_index("wide"), lax.axis_index("narrow")
    x, yl, c = w // 8, lax.rem(w // 2, 4), lax.rem(w, 2)
    z, yh = n // 2, lax.rem(n, 2)
    chip = w // 2
    partner = (w + 1 - 2 * c, n)
    across = (w, n + 1 - 2 * yh)

    owner = (yl == 1) | (yl == 2)

    def chip_at(dx, to_yl):
        return (lax.rem(x + dx, 4) * 8 + to_yl * 2 + c, n)

    def y_peer(d):
        y = lax.rem(yh * 4 + yl + d, 8)
        return (x * 8 + lax.rem(y, 4) * 2 + c, z * 2 + y // 4)

    def z_peer(d):
        return (w, lax.rem(n + 2 * d, 16))

    def narrow_peer(dz, dy):
        return (w, lax.rem(z + dz, 8) * 2 + lax.rem(yh + dy, 2))

    mine, other = pl.ds(pl.multiple_of(c * 32, 32), 32), pl.ds(pl.multiple_of(32 - c * 32, 32), 32)
    loads = [
        (qa_h.at[mine], qa.at[pl.ds(0, 32)]),
        (qa_h.at[other], qa.at[pl.ds(32, 32)]),
        (ab_h, ab),
        (qg_h.at[mine], qg.at[pl.ds(0, 32)]),
        (qg_h.at[other], qg.at[pl.ds(32, 32)]),
        (gb_h, gb),
        (tg_h, tg.at[0]),
        (eig_h, eig),
        (ta_h, ta),
    ]
    loads = [pltpu.make_async_copy(s, d, load.at[i]) for i, (s, d) in enumerate(loads)]
    for one in loads[:3]:
        one.start()

    barrier = pltpu.get_barrier_semaphore()

    def greet(peer):
        pl.semaphore_signal(barrier, inc=1, device_id=peer, device_id_type=MESH)

    for d in RING8:
        greet(z_peer(d))
    for d in RING4 + (0,):
        for e in (2, 1, 3, 0):
            if d or e:
                greet(chip_at(d, lax.rem(yl + e, 4)))
    greet(across)
    for e in (2, 1, 3):
        greet((w + 2 * (lax.rem(yl + e, 4) - yl), n + 1 - 2 * yh))
    greet(partner)

    def remote(src, dst, i, peer):
        pltpu.make_async_remote_copy(
            src, dst, send.at[i], recv.at[i], device_id=peer, device_id_type=MESH
        ).start()

    def await_bytes(ref, sem):
        pltpu.make_async_copy(ref, ref, sem).wait()

    for i in range(3):
        loads[i].wait()
    for one in loads[3:]:
        one.start()
    part = jnp.dot(qa[...], ab[...], preferred_element_type=F32)
    for k in range(16):
        rows, cols = 16 * (k // 8), slice(128 * (k % 8), 128 * (k % 8) + 128)
        keep[k] = part[rows : rows + 16, cols]
        ca_s[k] = part[rows + 32 : rows + 48, cols].astype(BF)
    pl.semaphore_wait(barrier, 27)
    remote(ca_s, ca_r, CA, partner)
    pl.semaphore_signal(ready, inc=1, device_id=across, device_id_type=MESH)
    for i in range(3, 6):
        loads[i].wait()
    part = jnp.dot(qg[...], gb[...], preferred_element_type=F32)
    for k in range(8):
        rows, cols = 16 * (k // 4), slice(128 * (k % 4), 128 * (k % 4) + 128)
        zg_s[k] = part[rows : rows + 16, cols].astype(BF)
        cg_s[k] = part[rows + 32 : rows + 48, cols].astype(BF)
    remote(cg_s, zg_s.at[pl.ds(8, 8)], CG, partner)
    await_bytes(ca_r, recv.at[CA])
    ha_s[...] = (keep[...] + ca_r[...].astype(F32)).astype(BF)
    for d in RING4 + (0,):
        for to in (1, 2):

            def to_owner(d=d, to=to):
                at = pl.ds(4 * lax.rem(x + d, 4) + 2 * to - 2, 2)
                slot = 4 * ((4 - d) % 4) + lax.rem(yl - to + 4, 4) - 1
                remote(ha_s.at[at], ha_r.at[slot], HR, chip_at(d, to))

            if d:
                to_owner()
            else:
                pl.when(yl != to)(to_owner)

    await_bytes(cg_s, recv.at[CG])
    for d in RING8:
        remote(zg_s.at[pl.ds(2 * lax.rem(z + d, 8), 2)], zg_r.at[d - 1], ZR, z_peer(d))

    loads[6].wait()
    remote(tg.at[0], tg.at[1], CT, partner)
    loads[7].wait()
    for k in range(2):
        inv[k] = (1.0 / eig[pl.ds(256 * k, 256), :]).astype(BF)
    remote(inv.at[pl.ds(0, 2)], inv.at[pl.ds(2, 2)], CI, partner)
    loads[8].wait()

    @pl.when(owner)
    def _():
        await_bytes(ha_r, recv.at[HR])
        at = pl.ds(4 * x + 2 * yl - 2, 2)
        rot_a[at] = (ha_s[at].astype(F32) + jnp.sum(ha_r[...].astype(F32), axis=0)).astype(BF)
        for d in RING4 + (0,):
            for e in (2, 1, 3, 0):
                if d or e:
                    remote(rot_a.at[at], rot_a.at[at], HG, chip_at(d, lax.rem(yl + e, 4)))

    await_bytes(zg_r, recv.at[ZR])
    own = pl.ds(2 * z, 2)
    held = pl.ds(16 * yh + 2 * z, 2)
    rot_g[held] = (zg_s[own].astype(F32) + jnp.sum(zg_r[...].astype(F32), axis=0)).astype(BF)
    pl.semaphore_wait(ready, 1)
    for e in (1, 0):
        for d in RING8 + (0,):
            if d or e:
                remote(rot_g.at[held], rot_g.at[held], NG, narrow_peer(d, e))

    await_bytes(tg.at[0], recv.at[CT])
    for k in range(2):
        tgf[:, 512 * k : 512 * k + 512] = tg[k].astype(F32)

    @pl.when(owner)
    def _():
        await_bytes(rot_a.at[pl.ds(0, 14)], recv.at[HG])

    @pl.when(jnp.logical_not(owner))
    def _():
        await_bytes(rot_a, recv.at[HG])

    for k in range(16):
        raf[16 * (k // 8) : 16 * (k // 8) + 16, 128 * (k % 8) : 128 * (k % 8) + 128] = rot_a[k].astype(F32)

    @pl.loop(0, 4)
    def _(b):
        for k in range(8):
            row = raf[pl.ds(b * 8 + k, 1), :]
            at = pl.multiple_of(b * 512 + k * 64, 64)
            for j in range(8):
                cols = slice(128 * j, 128 * j + 128)
                wide_row = jnp.broadcast_to(row[:, cols], (16, 128)).astype(BF)
                for t in range(4):
                    pairs[pl.ds(at + 16 * t, 16), cols] = wide_row * ta[16 * t : 16 * t + 16, cols]

    await_bytes(inv.at[pl.ds(0, 2)], recv.at[CI])

    def product(b):
        return lax.dot_general(
            pairs[...], inv[b], (((1,), (1,)), ((), ())), preferred_element_type=F32
        )

    @pl.loop(0, 3)
    def _(b):
        first[b] = product(b)

    await_bytes(rot_g.at[pl.ds(0, 30)], recv.at[NG])
    for k in range(16):
        rows, cols = 16 * (k // 4 % 2), 512 * (k // 8) + 128 * (k % 4)
        both = rot_g[k].astype(F32) + rot_g[16 + k].astype(F32)
        rgf[rows : rows + 16, cols : cols + 128] = both.astype(BF).astype(F32)

    final = product(3)
    for k in range(32):
        rows = slice(64 * k, 64 * k + 64)
        total = None
        for b in range(4):
            cols = slice(256 * b, 256 * b + 256)
            terms = (first[b, rows] if b < 3 else final[rows]) * tgf[:, cols] * rgf[k : k + 1, cols]
            terms = terms[:, :128] + terms[:, 128:]
            total = terms if total is None else total + terms
        accs[rows, :] = total

    ones = jnp.ones((8, 128), BF)
    high = accs[...].astype(BF)
    low = (accs[...] - high.astype(F32)).astype(BF)
    last = (((1,), (1,)), ((), ()))
    sums = lax.dot_general(ones, high, last, preferred_element_type=F32) + lax.dot_general(
        ones, low, last, preferred_element_type=F32
    )
    for k in range(16):
        s0[k : k + 1, :] = sums[0:1, 128 * k : 128 * k + 128]

    for d in RING4:
        remote(s0, xr.at[d - 1], AX, chip_at(d, yl))
    await_bytes(xr, recv.at[AX])
    s1[...] = s0[...] + jnp.sum(xr[...], axis=0)

    for d in RING8:
        remote(s1, yr.at[d - 1], AY, y_peer(d))

    await_bytes(yr, recv.at[AY])
    s2[...] = s1[...] + jnp.sum(yr[...], axis=0)

    for d in RING8:
        remote(s2, zr.at[d - 1], AZ, z_peer(d))

    await_bytes(zr, recv.at[AZ])
    s3[...] = (s2[...] + jnp.sum(zr[...], axis=0)) * float(A * G) ** (-0.5)
    remote(s3, fr, FC, partner)
    await_bytes(fr, recv.at[FC])
    out[pl.ds(pl.multiple_of(16 * c, 16), 16), :] = s3[...]
    out[pl.ds(pl.multiple_of(16 - 16 * c, 16), 16), :] = fr[...]

    sent = {
        CA: ca_s, CG: cg_s, CT: tg.at[0], CI: inv.at[pl.ds(0, 2)], ZR: zg_r,
        AX: xr, AY: yr, AZ: zr, FC: fr,
    }
    for i, ref in sent.items():
        await_bytes(ref, send.at[i])
    await_bytes(rot_g.at[pl.ds(0, 30)], send.at[NG])

    @pl.when(owner)
    def _():
        await_bytes(ha_s.at[pl.ds(0, 14)], send.at[HR])
        await_bytes(ha_r, send.at[HG])

    @pl.when(jnp.logical_not(owner))
    def _():
        await_bytes(ha_s, send.at[HR])


def on_device(*operands):
    vm = pltpu.VMEM
    scratch = [
        vm((64, 512), BF), vm((64, 1024), BF), vm((512, 1024), BF), vm((1024, 512), BF),
        vm((512, 1024), F32), vm((64, 1024), BF), vm((2, 64, 512), BF),
        vm((4, 256, 1024), BF), vm((16, 16, 128), F32), vm((16, 16, 128), BF), vm((16, 16, 128), BF),
        vm((16, 16, 128), BF), vm((15, 2, 16, 128), BF), vm((16, 16, 128), BF),
        vm((8, 16, 128), BF), vm((16, 16, 128), BF), vm((7, 2, 16, 128), BF),
        vm((32, 16, 128), BF),
        vm((32, 1024), F32), vm((32, 1024), F32), vm((64, 1024), F32),
        vm((2048, 1024), BF), vm((3, 2048, 256), F32), vm((2048, 128), F32),
        vm((16, 128), F32), vm((16, 128), F32), vm((16, 128), F32), vm((16, 128), F32),
        vm((3, 16, 128), F32), vm((7, 16, 128), F32), vm((7, 16, 128), F32), vm((16, 128), F32),
        pltpu.SemaphoreType.DMA((9,)),
        pltpu.SemaphoreType.DMA((N_EXCHANGES,)),
        pltpu.SemaphoreType.DMA((N_EXCHANGES,)),
        pltpu.SemaphoreType.REGULAR,
    ]
    scores = pl.pallas_call(
        kernel,
        out_shape=pltpu.VMEM((32, 128), F32),
        in_specs=[pl.BlockSpec(memory_space=pl.ANY)] * 7,
        out_specs=pl.BlockSpec(memory_space=pltpu.VMEM),
        scratch_shapes=scratch,
        compiler_params=pltpu.CompilerParams(
            collective_id=0, has_side_effects=True, vmem_limit_bytes=60 * 2**20
        ),
        name="influence",
    )(*operands)
    return scores.reshape(64, 64)


def solution(mesh):
    in_specs = (
        P(None, "wide"),
        P(None, "narrow"),
        P("wide", "narrow"),
        P("narrow", "wide"),
        P("wide", "narrow"),
        P(None, "narrow"),
        P(None, "wide"),
    )
    return jax.shard_map(on_device, mesh=mesh, in_specs=in_specs, out_specs=P(), check_vma=False)
```

```python
import jax
import jax.numpy as jnp
from jax import lax
from jax.experimental import pallas as pl
from jax.experimental.pallas import tpu as pltpu
from jax.sharding import PartitionSpec as P

A = 16384
G = 16384
BF = jnp.bfloat16
F32 = jnp.float32
MESH = pl.DeviceIdType.MESH

CA, CG, CT, CI, HR, HG, ZR, NG, AX, AY, AZ, FC = range(12)
N_EXCHANGES = 12
RING4 = (2, 1, 3)
RING8 = (4, 3, 5, 2, 6, 1, 7)


def kernel(
    qa_h, qg_h, ab_h, gb_h, eig_h, ta_h, tg_h,
    out,
    qa, qg, ab, gb, eig, ta, tg,
    inv, keep, ca_s, ca_r, ha_s, ha_r, rot_a, cg_s, zg_s, zg_r, rot_g,
    raf, rgf, tgf, pairs, first, accs, s0, s1, s2, s3, xr, yr, zr, fr,
    load, send, recv, ready,
):
    w, n = lax.axis_index("wide"), lax.axis_index("narrow")
    x, yl, c = w // 8, lax.rem(w // 2, 4), lax.rem(w, 2)
    z, yh = n // 2, lax.rem(n, 2)
    chip = w // 2
    partner = (w + 1 - 2 * c, n)
    across = (w, n + 1 - 2 * yh)

    owner = (yl == 1) | (yl == 2)

    def chip_at(dx, to_yl):
        return (lax.rem(x + dx, 4) * 8 + to_yl * 2 + c, n)

    def y_peer(d):
        y = lax.rem(yh * 4 + yl + d, 8)
        return (x * 8 + lax.rem(y, 4) * 2 + c, z * 2 + y // 4)

    def z_peer(d):
        return (w, lax.rem(n + 2 * d, 16))

    def narrow_peer(dz, dy):
        return (w, lax.rem(z + dz, 8) * 2 + lax.rem(yh + dy, 2))

    mine, other = pl.ds(pl.multiple_of(c * 32, 32), 32), pl.ds(pl.multiple_of(32 - c * 32, 32), 32)
    loads = [
        (qa_h.at[mine], qa.at[pl.ds(0, 32)]),
        (qa_h.at[other], qa.at[pl.ds(32, 32)]),
        (ab_h, ab),
        (qg_h.at[mine], qg.at[pl.ds(0, 32)]),
        (qg_h.at[other], qg.at[pl.ds(32, 32)]),
        (gb_h, gb),
        (tg_h, tg.at[0]),
        (eig_h, eig),
        (ta_h, ta),
    ]
    loads = [pltpu.make_async_copy(s, d, load.at[i]) for i, (s, d) in enumerate(loads)]
    for one in loads[:3]:
        one.start()

    barrier = pltpu.get_barrier_semaphore()

    def greet(peer):
        pl.semaphore_signal(barrier, inc=1, device_id=peer, device_id_type=MESH)

    for d in RING8:
        greet(z_peer(d))
    for d in RING4 + (0,):
        for e in (2, 1, 3, 0):
            if d or e:
                greet(chip_at(d, lax.rem(yl + e, 4)))
    greet(across)
    for e in (2, 1, 3):
        greet((w + 2 * (lax.rem(yl + e, 4) - yl), n + 1 - 2 * yh))
    greet(partner)

    def remote(src, dst, i, peer):
        pltpu.make_async_remote_copy(
            src, dst, send.at[i], recv.at[i], device_id=peer, device_id_type=MESH
        ).start()

    def await_bytes(ref, sem):
        pltpu.make_async_copy(ref, ref, sem).wait()

    for i in range(3):
        loads[i].wait()
    for one in loads[3:]:
        one.start()
    part = jnp.dot(qa[...], ab[...], preferred_element_type=F32)
    for k in range(16):
        rows, cols = 16 * (k // 8), slice(128 * (k % 8), 128 * (k % 8) + 128)
        keep[k] = part[rows : rows + 16, cols]
        ca_s[k] = part[rows + 32 : rows + 48, cols].astype(BF)
    pl.semaphore_wait(barrier, 27)
    remote(ca_s, ca_r, CA, partner)
    pl.semaphore_signal(ready, inc=1, device_id=across, device_id_type=MESH)
    for i in range(3, 6):
        loads[i].wait()
    part = jnp.dot(qg[...], gb[...], preferred_element_type=F32)
    for k in range(8):
        rows, cols = 16 * (k // 4), slice(128 * (k % 4), 128 * (k % 4) + 128)
        zg_s[k] = part[rows : rows + 16, cols].astype(BF)
        cg_s[k] = part[rows + 32 : rows + 48, cols].astype(BF)
    remote(cg_s, zg_s.at[pl.ds(8, 8)], CG, partner)
    await_bytes(ca_r, recv.at[CA])
    ha_s[...] = (keep[...] + ca_r[...].astype(F32)).astype(BF)
    for d in RING4 + (0,):
        for to in (1, 2):

            def to_owner(d=d, to=to):
                at = pl.ds(4 * lax.rem(x + d, 4) + 2 * to - 2, 2)
                slot = 4 * ((4 - d) % 4) + lax.rem(yl - to + 4, 4) - 1
                remote(ha_s.at[at], ha_r.at[slot], HR, chip_at(d, to))

            if d:
                to_owner()
            else:
                pl.when(yl != to)(to_owner)

    await_bytes(cg_s, recv.at[CG])
    for d in RING8:
        remote(zg_s.at[pl.ds(2 * lax.rem(z + d, 8), 2)], zg_r.at[d - 1], ZR, z_peer(d))

    loads[6].wait()
    remote(tg.at[0], tg.at[1], CT, partner)
    loads[7].wait()
    for k in range(2):
        inv[k] = (1.0 / eig[pl.ds(256 * k, 256), :]).astype(BF)
    remote(inv.at[pl.ds(0, 2)], inv.at[pl.ds(2, 2)], CI, partner)
    loads[8].wait()

    await_bytes(tg.at[0], recv.at[CT])
    for k in range(2):
        tgf[:, 512 * k : 512 * k + 512] = tg[k].astype(F32)

    @pl.when(owner)
    def _():
        await_bytes(ha_r, recv.at[HR])
        at = pl.ds(4 * x + 2 * yl - 2, 2)
        rot_a[at] = (ha_s[at].astype(F32) + jnp.sum(ha_r[...].astype(F32), axis=0)).astype(BF)
        for d in RING4 + (0,):
            for e in (2, 1, 3, 0):
                if d or e:
                    remote(rot_a.at[at], rot_a.at[at], HG, chip_at(d, lax.rem(yl + e, 4)))

    await_bytes(zg_r, recv.at[ZR])
    own = pl.ds(2 * z, 2)
    held = pl.ds(16 * yh + 2 * z, 2)
    rot_g[held] = (zg_s[own].astype(F32) + jnp.sum(zg_r[...].astype(F32), axis=0)).astype(BF)
    pl.semaphore_wait(ready, 1)
    for e in (1, 0):
        for d in RING8 + (0,):
            if d or e:
                remote(rot_g.at[held], rot_g.at[held], NG, narrow_peer(d, e))

    @pl.when(owner)
    def _():
        await_bytes(rot_a.at[pl.ds(0, 14)], recv.at[HG])

    @pl.when(jnp.logical_not(owner))
    def _():
        await_bytes(rot_a, recv.at[HG])

    for k in range(16):
        raf[16 * (k // 8) : 16 * (k // 8) + 16, 128 * (k % 8) : 128 * (k % 8) + 128] = rot_a[k].astype(F32)

    await_bytes(inv.at[pl.ds(0, 2)], recv.at[CI])

    for k in range(32):
        row = raf[k : k + 1, :]
        for j in range(8):
            cols = slice(128 * j, 128 * j + 128)
            wide_row = jnp.broadcast_to(row[:, cols], (16, 128)).astype(BF)
            for t in range(4):
                at = 64 * k + 16 * t
                pairs[at : at + 16, cols] = wide_row * ta[16 * t : 16 * t + 16, cols]

    def product(b):
        return lax.dot_general(
            pairs[...], inv[b], (((1,), (1,)), ((), ())), preferred_element_type=F32
        )

    first[0] = product(0)

    @pl.loop(1, 4)
    def _(b):
        first[b] = product(b)

    await_bytes(rot_g.at[pl.ds(0, 30)], recv.at[NG])
    for k in range(16):
        rows, cols = 16 * (k // 4 % 2), 512 * (k // 8) + 128 * (k % 4)
        both = rot_g[k].astype(F32) + rot_g[16 + k].astype(F32)
        rgf[rows : rows + 16, cols : cols + 128] = both.astype(BF).astype(F32)

    @pl.loop(0, 8)
    def _(g):
        for k in range(4):
            rows = pl.ds(pl.multiple_of(256 * g + 64 * k, 64), 64)
            total = None
            for b in range(4):
                cols = slice(256 * b, 256 * b + 256)
                terms = first[b, rows] * tgf[:, cols] * rgf[pl.ds(4 * g + k, 1), cols]
                terms = terms[:, :128] + terms[:, 128:]
                total = terms if total is None else total + terms
            accs[rows, :] = total

    ones = jnp.ones((8, 128), BF)
    high = accs[...].astype(BF)
    low = (accs[...] - high.astype(F32)).astype(BF)
    last = (((1,), (1,)), ((), ()))
    sums = lax.dot_general(ones, high, last, preferred_element_type=F32) + lax.dot_general(
        ones, low, last, preferred_element_type=F32
    )
    for k in range(16):
        s0[k : k + 1, :] = sums[0:1, 128 * k : 128 * k + 128]

    for d in RING4:
        remote(s0, xr.at[d - 1], AX, chip_at(d, yl))
    await_bytes(xr, recv.at[AX])
    s1[...] = s0[...] + jnp.sum(xr[...], axis=0)

    for d in RING8:
        remote(s1, yr.at[d - 1], AY, y_peer(d))

    await_bytes(yr, recv.at[AY])
    s2[...] = s1[...] + jnp.sum(yr[...], axis=0)

    for d in RING8:
        remote(s2, zr.at[d - 1], AZ, z_peer(d))

    await_bytes(zr, recv.at[AZ])
    s3[...] = (s2[...] + jnp.sum(zr[...], axis=0)) * float(A * G) ** (-0.5)
    remote(s3, fr, FC, partner)
    await_bytes(fr, recv.at[FC])
    out[pl.ds(pl.multiple_of(16 * c, 16), 16), :] = s3[...]
    out[pl.ds(pl.multiple_of(16 - 16 * c, 16), 16), :] = fr[...]

    sent = {
        CA: ca_s, CG: cg_s, CT: tg.at[0], CI: inv.at[pl.ds(0, 2)], ZR: zg_r,
        AX: xr, AY: yr, AZ: zr, FC: fr,
    }
    for i, ref in sent.items():
        await_bytes(ref, send.at[i])
    await_bytes(rot_g.at[pl.ds(0, 30)], send.at[NG])

    @pl.when(owner)
    def _():
        await_bytes(ha_s.at[pl.ds(0, 14)], send.at[HR])
        await_bytes(ha_r, send.at[HG])

    @pl.when(jnp.logical_not(owner))
    def _():
        await_bytes(ha_s, send.at[HR])


def on_device(*operands):
    vm = pltpu.VMEM
    scratch = [
        vm((64, 512), BF), vm((64, 1024), BF), vm((512, 1024), BF), vm((1024, 512), BF),
        vm((512, 1024), F32), vm((64, 1024), BF), vm((2, 64, 512), BF),
        vm((4, 256, 1024), BF), vm((16, 16, 128), F32), vm((16, 16, 128), BF), vm((16, 16, 128), BF),
        vm((16, 16, 128), BF), vm((15, 2, 16, 128), BF), vm((16, 16, 128), BF),
        vm((8, 16, 128), BF), vm((16, 16, 128), BF), vm((7, 2, 16, 128), BF),
        vm((32, 16, 128), BF),
        vm((32, 1024), F32), vm((32, 1024), F32), vm((64, 1024), F32),
        vm((2048, 1024), BF), vm((4, 2048, 256), F32), vm((2048, 128), F32),
        vm((16, 128), F32), vm((16, 128), F32), vm((16, 128), F32), vm((16, 128), F32),
        vm((3, 16, 128), F32), vm((7, 16, 128), F32), vm((7, 16, 128), F32), vm((16, 128), F32),
        pltpu.SemaphoreType.DMA((9,)),
        pltpu.SemaphoreType.DMA((N_EXCHANGES,)),
        pltpu.SemaphoreType.DMA((N_EXCHANGES,)),
        pltpu.SemaphoreType.REGULAR,
    ]
    scores = pl.pallas_call(
        kernel,
        out_shape=pltpu.VMEM((32, 128), F32),
        in_specs=[pl.BlockSpec(memory_space=pl.ANY)] * 7,
        out_specs=pl.BlockSpec(memory_space=pltpu.VMEM),
        scratch_shapes=scratch,
        compiler_params=pltpu.CompilerParams(
            collective_id=0, has_side_effects=True, vmem_limit_bytes=60 * 2**20
        ),
        name="influence",
    )(*operands)
    return scores.reshape(64, 64)


def solution(mesh):
    in_specs = (
        P(None, "wide"),
        P(None, "narrow"),
        P("wide", "narrow"),
        P("narrow", "wide"),
        P("wide", "narrow"),
        P(None, "narrow"),
        P(None, "wide"),
    )
    return jax.shard_map(on_device, mesh=mesh, in_specs=in_specs, out_specs=P(), check_vma=False)
```
